128 devices in a mesh: dp: 32 (over x, y_lo, z), outer: 4 (over y_hi, core).
Axes of the slice: x: 4, y: 4 (y_hi: 2, y_lo: 2; y = y_hi * 2 + y_lo), z: 4, core: 2. Of those that a mesh axis runs over, the one named last changes fastest.
Arguments:
- tokens: bfloat16 [65536, 4096], P(('dp', 'outer')), may hold values from -6 to 6
- grad_out: bfloat16 [65536, 11008], P(('dp', 'outer')), may hold values from -0.0234375 to 0.0234375
- projection_basis: bfloat16 [4096, 512], replicated, may hold values from -0.09375 to 0.09375
- first_moment: float32 [512, 11008], P(('dp', 'outer')), may hold values from -3 to 3
- second_moment: float32 [512, 11008], P(('dp', 'outer')), may hold values from 0.2 to 4
Outputs:
- weight_update: float32 [4096, 11008], P('dp')
- new_first: float32 [512, 11008], P(('dp', 'outer'))
- new_second: float32 [512, 11008], P(('dp', 'outer'))
The draws below stay inside these ranges and needn't reach their ends.
All inputs are finite; a program needn't handle non-finite values.
Results may differ from the reference program's by a relative error of at most 0.003.
Values may be sent and summed in bfloat16 or wider, within the bound.
No kernel may reach another device: no remote copies, remote signals or barrier semaphores. Data moves between devices by JAX's collectives and lax.ppermute only.
A program may use at most 192 MiB of HBM per device.

```python
import math
import jax
import jax.numpy as jnp

D = 4096
FF = 11008
R = 512
STEP = 100
TOKENS = 65536


def level_of(key, dims, shards, low, high):
    def one(dim, shards_of):
        steps = jax.random.uniform(jax.random.fold_in(jax.random.fold_in(key, 6), dim), (shards_of,), jnp.float32, low / len(shards), high / len(shards))
        return jnp.repeat(jnp.exp(steps), dims[dim] // shards_of).reshape((-1,) + (1,) * (len(dims) - dim - 1))

    level = one(*shards[0])
    for cut in shards[1:]:
        level = level * one(*cut)
    return level


def gaussian(stream_key, extent, spread, reach, split=(), held_as=jnp.bfloat16):
    entries = jax.random.normal(stream_key, extent, jnp.float32) * spread
    if len(split) > 0:
        entries = level_of(stream_key, extent, split, -0.22, 0.18) * entries
    return jnp.clip(entries, min=-reach, max=reach).astype(held_as)


def setup_inputs(seed: int = 0) -> dict:
    streams_of = jax.random.split(jax.random.key(seed), 6)
    tokens = gaussian(streams_of[0], (TOKENS, D), 1.0, 6.0, ((0, 128),))
    grad_out = gaussian(streams_of[1], (TOKENS, FF), TOKENS ** -0.5, 0.0234375, ((0, 128),))
    projection_basis = gaussian(streams_of[2], (D, R), D ** -0.5, 0.09375)
    first_moment = gaussian(streams_of[3], (R, FF), 0.5, 3.0, ((0, 128),), jnp.float32)
    second_moment = jnp.clip(jnp.exp(math.log(4.0) - 2.9957323 * jax.random.uniform(streams_of[4], (R, FF), jnp.float32) ** level_of(streams_of[4], (R, FF), ((0, 128),), -0.2, 0.2)), 0.2, 4.0)
    return {"tokens": tokens, "grad_out": grad_out, "projection_basis": projection_basis, "first_moment": first_moment, "second_moment": second_moment}


beta_first = 0.9
beta_second = 0.999
epsilon = 1e-08
galore_scale = 0.25

def reference(tokens, grad_out, projection_basis, first_moment, second_moment):
    projected = jnp.dot(tokens, projection_basis, preferred_element_type=jnp.float32).astype(jnp.bfloat16)
    grad_low = jnp.dot(projected.T, grad_out, preferred_element_type=jnp.float32)
    new_first = beta_first * first_moment + (1.0 - beta_first) * grad_low
    new_second = beta_second * second_moment + (1.0 - beta_second) * grad_low * grad_low
    first_bias = 1.0 - beta_first ** STEP
    second_bias = 1.0 - beta_second ** STEP
    low_update = (new_first / first_bias / (jnp.sqrt(new_second / second_bias) + epsilon)).astype(jnp.bfloat16)
    weight_update = -galore_scale * jnp.dot(projection_basis, low_update, preferred_element_type=jnp.float32)
    return (weight_update, new_first, new_second)
```

```python
import itertools

import jax
import jax.numpy as jnp
from jax import lax
from jax.experimental import pallas as pl
from jax.experimental.pallas import tpu as pltpu
from jax.sharding import PartitionSpec as P

STEP = 100

beta_first = 0.9
beta_second = 0.999
epsilon = 1e-08
galore_scale = 0.25

AXES = ("dp", "outer")
WIDTH = 1280
PIECES = ((0, 3840), (3840, 3840), (7680, 3328))
ORDERS = ((0, 1, 2), (1, 2, 0), (2, 0, 1))


def linear(x, y, z, core):
    return ((((x % 4) * 2 + y % 2) * 4 + z % 4) * 2 + (y % 4) // 2) * 2 + core


def ring(axis, sign):
    pairs = []
    for x, y, z, core in itertools.product(range(4), range(4), range(4), range(2)):
        there = [x, y, z]
        there[axis] += sign * (1 - 2 * core)
        pairs.append((linear(x, y, z, core), linear(*there, core)))
    return pairs


SWAP = [(2 * i + core, 2 * i + 1 - core) for i in range(64) for core in range(2)]
UP = [ring(axis, 1) for axis in range(3)]
DOWN = [ring(axis, -1) for axis in range(3)]


def send(value, pairs):
    return lax.ppermute(value, AXES, pairs)


def rank_order(order, dp, outer):
    here = (dp // 8, (outer // 2) * 2 + (dp // 4) % 2, dp % 4)
    place = lax.iota(jnp.int32, 512)
    hops = (place // 128, (place // 16) % 4, (place // 4) % 4)
    core = (outer % 2 + (place // 64) % 2) % 2
    there = [None, None, None]
    for hop, axis in zip(hops, order):
        there[axis] = (here[axis] + 4 + (1 - 2 * core) * hop) % 4
    return linear(*there, core) * 4 + place % 4


def term_kernel(projected_ref, grad_ref, own_ref, other_ref):
    total = jnp.dot(projected_ref[...], grad_ref[...], preferred_element_type=jnp.float32)
    own_ref[...] = total[:64].astype(jnp.bfloat16)
    other_ref[...] = total[64:].astype(jnp.bfloat16)


def term_rows(projected, grad_out, hop):
    tokens, width = grad_out.shape
    shape = jax.ShapeDtypeStruct((64, width), jnp.bfloat16)
    block = pl.BlockSpec((64, WIDTH), lambda j: (0, j))
    return pl.pallas_call(
        term_kernel,
        grid=(pl.cdiv(width, WIDTH),),
        in_specs=[
            pl.BlockSpec((128, tokens), lambda j: (j // 3 * 4 + hop, 0)),
            pl.BlockSpec((tokens, WIDTH), lambda j: (0, j)),
        ],
        out_specs=[block, block],
        out_shape=[shape, shape],
        cost_estimate=pl.CostEstimate(
            flops=2 * 128 * tokens * width,
            bytes_accessed=2 * (tokens + 128) * width,
            transcendentals=0,
        ),
        name="terms",
    )(projected, grad_out)


def expand_kernel(basis_ref, *refs):
    out_ref = refs[-1]
    step = pl.program_id(0)
    for piece in range(3):

        @pl.when(step // 3 == piece)
        def _(piece=piece):
            low = jnp.concatenate([ref[...] for ref in refs[8 * piece : 8 * piece + 8]], axis=0)
            out_ref[...] = -galore_scale * jnp.dot(
                basis_ref[...], low, preferred_element_type=jnp.float32
            )


def expand(basis_rows, blocks, width):
    rows = basis_rows.shape[0]
    specs = []
    for piece in range(3):
        spec = pl.BlockSpec((64, WIDTH), lambda j, piece=piece: (0, jnp.clip(j - 3 * piece, 0, 2)))
        specs += [spec] * 8
    return pl.pallas_call(
        expand_kernel,
        grid=(pl.cdiv(width, WIDTH),),
        in_specs=[pl.BlockSpec((rows, 512), lambda j: (0, j // 3))] + specs,
        out_specs=pl.BlockSpec((rows, WIDTH), lambda j: (0, j)),
        out_shape=jax.ShapeDtypeStruct((rows, width), jnp.float32),
        cost_estimate=pl.CostEstimate(
            flops=2 * rows * 512 * width,
            bytes_accessed=(2 * 512 + 4 * rows) * width,
            transcendentals=0,
        ),
        compiler_params=pltpu.CompilerParams(vmem_limit_bytes=48 * 1024 * 1024),
        name="expand",
    )(basis_rows, *itertools.chain(*blocks))


def shards(tokens, grad_out, projection_basis, first_moment, second_moment):
    width = grad_out.shape[1]
    dp, outer = lax.axis_index("dp"), lax.axis_index("outer")
    f32, bf16 = jnp.float32, jnp.bfloat16

    places = jnp.concatenate([rank_order(order, dp, outer) for order in ORDERS])
    picks = (lax.broadcasted_iota(jnp.int32, (512, 1536), 0) == places[None, :]).astype(bf16)

    projected = jnp.dot(tokens, projection_basis, preferred_element_type=f32).astype(bf16)
    projected = lax.dot_general(
        picks, projected, (((0,), (1,)), ((), ())), preferred_element_type=f32
    ).astype(bf16)
    local_width = projection_basis.shape[0] // 32
    basis_rows = lax.dynamic_slice_in_dim(projection_basis, dp * local_width, local_width, 0)
    basis_rows = jnp.dot(basis_rows, picks, preferred_element_type=f32).astype(bf16)

    sums = [None] * 3
    for hop in (3, 2, 1, 0):
        own, other = term_rows(projected, grad_out, hop)
        other = send(other, SWAP)
        for piece, (start, size) in enumerate(PIECES):
            total = own[:, start : start + size].astype(f32) + other[:, start : start + size].astype(f32)
            if hop < 3:
                total = total + send(sums[piece], UP[ORDERS[piece][0]]).astype(f32)
            sums[piece] = total.astype(bf16) if hop else total
    for stage, rows, kind in ((1, 16, bf16), (2, 4, f32)):
        held = sums
        sums = [h[3 * rows :].astype(kind) for h in held]
        for hop in (2, 1, 0):
            for piece in range(3):
                total = held[piece][hop * rows : (hop + 1) * rows] + send(
                    sums[piece], UP[ORDERS[piece][stage]]
                ).astype(f32)
                sums[piece] = total.astype(kind) if hop else total
    owned_grad = jnp.concatenate(sums, axis=1)

    new_first = beta_first * first_moment + (1.0 - beta_first) * owned_grad
    new_second = beta_second * second_moment + (1.0 - beta_second) * owned_grad * owned_grad
    first_bias = 1.0 - beta_first**STEP
    second_bias = 1.0 - beta_second**STEP
    low_update = (new_first / first_bias / (jnp.sqrt(new_second / second_bias) + epsilon)).astype(bf16)

    low = [low_update[:, start : start + size] for start, size in PIECES]
    for stage in (2, 1, 0):
        parts = [[value] for value in low]
        for _ in range(3):
            for piece in range(3):
                parts[piece].append(send(parts[piece][-1], DOWN[ORDERS[piece][stage]]))
        if stage:
            low = [jnp.concatenate(p, axis=0) for p in parts]
    blocks = [
        [block for part in parts[piece] for block in (part, send(part, SWAP))] for piece in range(3)
    ]
    weight_update = expand(basis_rows, blocks, width)
    return (weight_update, new_first, new_second)


def solution(mesh):
    in_specs = (
        P(("dp", "outer"), None),
        P(("dp", "outer"), None),
        P(),
        P(("dp", "outer"), None),
        P(("dp", "outer"), None),
    )
    out_specs = (P("dp", None), P(("dp", "outer"), None), P(("dp", "outer"), None))
    return jax.shard_map(shards, mesh=mesh, in_specs=in_specs, out_specs=out_specs, check_vma=False)
```

```python
import itertools

import jax
import jax.numpy as jnp
from jax import lax
from jax.experimental import pallas as pl
from jax.experimental.pallas import tpu as pltpu
from jax.sharding import PartitionSpec as P

STEP = 100

beta_first = 0.9
beta_second = 0.999
epsilon = 1e-08
galore_scale = 0.25

AXES = ("dp", "outer")
WIDTH = 1280
PIECES = ((0, 3840), (3840, 3840), (7680, 3328))
X, Y, Z = 0, 1, 2
BITS = (
    ((X, 0), (Z, 0), (Y, 0), (Z, 1)),
    ((Y, 0), (X, 0), (Z, 1), (Z, 0)),
    ((Z, 0), (Y, 0), (X, 0), (Z, 1)),
)
LAST = ((X, 1), (Y, 1))


def linear(x, y, z, core):
    return (((x * 2 + y % 2) * 4 + z) * 2 + y // 2) * 2 + core


def code(second, core):
    return 1 + 2 * ((second + core) % 2)


def exchange(*bits):
    pairs = []
    for x, y, z, core in itertools.product(range(4), range(4), range(4), range(2)):
        there = [x, y, z]
        for axis, second in bits:
            there[axis] ^= code(second, core)
        pairs.append((linear(x, y, z, core), linear(*there, core)))
    return pairs


SWAP = [(2 * i + core, 2 * i + 1 - core) for i in range(64) for core in range(2)]
QUAD = (exchange(LAST[1]), exchange(LAST[0]), exchange(*LAST))


def send(value, pairs):
    return lax.ppermute(value, AXES, pairs)


def send_pieces(values, level):
    values = lax.optimization_barrier(tuple(values))
    return lax.optimization_barrier(
        tuple(send(v, exchange(bits[level])) for v, bits in zip(values, BITS))
    )


def rank_order(bits, dp, outer):
    here = (dp // 8, (outer // 2) * 2 + (dp // 4) % 2, dp % 4)
    place = lax.iota(jnp.int32, 512)
    core = (outer + place // 256) % 2
    there = list(here)
    for level, (axis, second) in enumerate(bits + LAST):
        there[axis] = there[axis] ^ ((place // (128 >> level)) % 2 * code(second, core))
    return linear(*there, core) * 4 + place % 4


def expand_kernel(basis_ref, *refs):
    low = jnp.concatenate([ref[...] for ref in refs[:8]], axis=0)
    product = jnp.dot(basis_ref[...], low, preferred_element_type=jnp.float32)
    refs[-1][...] = -galore_scale * product


def expand(piece, basis_rows, blocks, width, *done):
    rows, (start, size) = basis_rows.shape[0], PIECES[piece]
    return pl.pallas_call(
        expand_kernel,
        grid=(pl.cdiv(size, WIDTH),),
        in_specs=[pl.BlockSpec((rows, 512), lambda j: (0, piece))]
        + [pl.BlockSpec((64, WIDTH), lambda j: (0, j))] * 8
        + [pl.BlockSpec(memory_space=pl.ANY)] * len(done),
        out_specs=pl.BlockSpec((rows, WIDTH), lambda j: (0, start // WIDTH + j)),
        out_shape=jax.ShapeDtypeStruct((rows, width), jnp.float32),
        input_output_aliases={9: 0} if done else {},
        cost_estimate=pl.CostEstimate(
            flops=2 * rows * 512 * size,
            bytes_accessed=(2 * 512 + 4 * rows) * size,
            transcendentals=0,
        ),
        compiler_params=pltpu.CompilerParams(vmem_limit_bytes=12 * 1024 * 1024),
        name="expand",
    )(basis_rows, *blocks, *done)


def shards(tokens, grad_out, projection_basis, first_moment, second_moment):
    dp, outer = lax.axis_index("dp"), lax.axis_index("outer")
    f32, bf16 = jnp.float32, jnp.bfloat16

    places = jnp.concatenate([rank_order(bits, dp, outer) for bits in BITS])
    picks = (lax.broadcasted_iota(jnp.int32, (512, 1536), 0) == places[None, :]).astype(bf16)

    projected = jnp.dot(tokens, projection_basis, preferred_element_type=f32).astype(bf16)
    projected = jnp.dot(projected, picks, preferred_element_type=f32).astype(bf16)
    local_width = projection_basis.shape[0] // 32
    basis_rows = lax.dynamic_slice_in_dim(projection_basis, dp * local_width, local_width, 0)
    basis_rows = jnp.dot(basis_rows, picks, preferred_element_type=f32).astype(bf16)

    own, other = [], []
    for piece, (start, size) in enumerate(PIECES):
        terms = lax.dot_general(
            projected[:, 512 * piece : 512 * piece + 512],
            grad_out[:, start : start + size],
            (((0,), (0,)), ((), ())),
            preferred_element_type=f32,
        ).astype(bf16)
        own.append(terms[:256])
        other.append(terms[256:])
    sent = [o[128:].astype(f32) + send(t[128:], SWAP).astype(f32) for o, t in zip(own, other)]
    held = [o[:128].astype(f32) + send(t[:128], SWAP).astype(f32) for o, t in zip(own, other)]
    for level in range(4):
        got = send_pieces([s.astype(bf16) for s in sent], level)
        held = [h + g.astype(f32) for h, g in zip(held, got)]
        half = held[0].shape[0] // 2
        if level < 3:
            sent, held = [h[half:] for h in held], [h[:half] for h in held]
    held = jnp.concatenate(held, axis=1)
    owned_grad = held[:4]
    for i, pairs in enumerate(QUAD):
        owned_grad = owned_grad + send(held[4 * i + 4 : 4 * i + 8], pairs)

    new_first = beta_first * first_moment + (1.0 - beta_first) * owned_grad
    new_second = beta_second * second_moment + (1.0 - beta_second) * owned_grad * owned_grad
    first_bias = 1.0 - beta_first**STEP
    second_bias = 1.0 - beta_second**STEP
    low_update = (new_first / first_bias / (jnp.sqrt(new_second / second_bias) + epsilon)).astype(bf16)

    low = jnp.concatenate([low_update] + [send(low_update, pairs) for pairs in QUAD], axis=0)
    low = [low[:, start : start + size] for start, size in PIECES]
    for level in (3, 2):
        got = send_pieces(low, level)
        low = [jnp.concatenate([mine, theirs], axis=0) for mine, theirs in zip(low, got)]
    blocks = [low, send_pieces(low, 1), send_pieces(low, 0)]
    blocks.append(send_pieces(blocks[1], 0))
    done = ()
    for piece in range(3):
        mine = [block[piece] for block in blocks]
        done = (expand(piece, basis_rows, mine + [send(m, SWAP) for m in mine], grad_out.shape[1], *done),)
    weight_update = done[0]
    return (weight_update, new_first, new_second)


def solution(mesh):
    in_specs = (
        P(("dp", "outer"), None),
        P(("dp", "outer"), None),
        P(),
        P(("dp", "outer"), None),
        P(("dp", "outer"), None),
    )
    out_specs = (P("dp", None), P(("dp", "outer"), None), P(("dp", "outer"), None))
    return jax.shard_map(shards, mesh=mesh, in_specs=in_specs, out_specs=out_specs, check_vma=False)
```

```python
import itertools

import jax
import jax.numpy as jnp
from jax import lax
from jax.experimental import pallas as pl
from jax.experimental.pallas import tpu as pltpu
from jax.sharding import PartitionSpec as P

STEP = 100

beta_first = 0.9
beta_second = 0.999
epsilon = 1e-08
galore_scale = 0.25

AXES = ("dp", "outer")
WIDTH = 3840
PIECES = ((0, 3840), (3840, 3840), (7680, 3328))
X, Y, Z = 0, 1, 2
BITS = (
    ((X, 0), (Z, 0), (Y, 0)),
    ((Y, 0), (X, 0), (Z, 0)),
    ((Z, 0), (Y, 0), (X, 0)),
)
LAST = ((X, 1), (Y, 1), (Z, 1))


def linear(x, y, z, core):
    return (((x * 2 + y % 2) * 4 + z) * 2 + y // 2) * 2 + core


def code(second, core):
    return 1 + 2 * ((second + core) % 2)


def exchange(*bits):
    pairs = []
    for x, y, z, core in itertools.product(range(4), range(4), range(4), range(2)):
        there = [x, y, z]
        for axis, second in bits:
            there[axis] ^= code(second, core)
        pairs.append((linear(x, y, z, core), linear(*there, core)))
    return pairs


SWAP = [(2 * i + core, 2 * i + 1 - core) for i in range(64) for core in range(2)]


def groups():
    found = []
    for x, y, z, core in itertools.product(range(4), range(4), range(4), range(2)):
        last = code(1, core)
        if all(at < at ^ last for at in (x, y, z)):
            corners = itertools.product((0, last), repeat=3)
            found.append([linear(x ^ dx, y ^ dy, z ^ dz, core) for dx, dy, dz in corners])
    return found


def swap_groups(value):
    return lax.all_to_all(value, AXES, 0, 0, axis_index_groups=groups(), tiled=True)


def send(value, pairs):
    return lax.ppermute(value, AXES, pairs)


def send_pieces(values, level):
    values = lax.optimization_barrier(tuple(values))
    return lax.optimization_barrier(
        tuple(send(v, exchange(bits[level])) for v, bits in zip(values, BITS))
    )


def rank_order(bits, dp, outer):
    here = (dp // 8, (outer // 2) * 2 + (dp // 4) % 2, dp % 4)
    place = lax.iota(jnp.int32, 512)
    core = (outer + place // 256) % 2
    there = list(here)
    for level, (axis, second) in enumerate(bits):
        there[axis] = there[axis] ^ ((place // (128 >> level)) % 2 * code(second, core))
    for level, (axis, second) in enumerate(LAST):
        last = code(second, core)
        first = jnp.minimum(there[axis], there[axis] ^ last)
        there[axis] = first ^ ((place // (16 >> level)) % 2 * last)
    return linear(*there, core) * 4 + place % 4


def project_kernel(tokens_ref, basis_ref, out_ref, total_ref):
    step = pl.program_id(0)
    product = jnp.dot(tokens_ref[...], basis_ref[...], preferred_element_type=jnp.float32)

    @pl.when(step == 0)
    def _():
        total_ref[...] = product

    @pl.when(step > 0)
    def _():
        total_ref[...] += product

    @pl.when(step == pl.num_programs(0) - 1)
    def _():
        out_ref[...] = total_ref[...].astype(jnp.bfloat16)


def project(tokens, basis, depth=1024):
    rows, width = tokens.shape[0], basis.shape[1]
    return pl.pallas_call(
        project_kernel,
        grid=(basis.shape[0] // depth,),
        in_specs=[
            pl.BlockSpec((rows, depth), lambda k: (0, k)),
            pl.BlockSpec((depth, width), lambda k: (k, 0)),
        ],
        out_specs=pl.BlockSpec((rows, width), lambda k: (0, 0)),
        out_shape=jax.ShapeDtypeStruct((rows, width), jnp.bfloat16),
        scratch_shapes=[pltpu.VMEM((rows, width), jnp.float32)],
        cost_estimate=pl.CostEstimate(
            flops=2 * rows * basis.shape[0] * width,
            bytes_accessed=2 * (rows + width) * basis.shape[0],
            transcendentals=0,
        ),
        compiler_params=pltpu.CompilerParams(vmem_limit_bytes=8 * 1024 * 1024),
        name="project",
    )(tokens, basis)


def expand_kernel(basis_ref, *refs):
    for piece in range(3):

        @pl.when(pl.program_id(0) == piece)
        def _(piece=piece):
            size = PIECES[piece][1]
            low = jnp.concatenate([refs[piece][...], refs[3 + piece][...]], axis=0)
            product = jnp.dot(basis_ref[...], low, preferred_element_type=jnp.float32)
            if len(refs) == 8:
                product = -galore_scale * (refs[6][:, :size] + product)
            refs[-1][:, :size] = product


def expand(basis_rows, own, other, *early):
    rows, depth, width = basis_rows.shape[0], 2 * own[0].shape[0], sum(size for _, size in PIECES)
    total = pl.BlockSpec((rows, WIDTH), lambda j: (0, j))
    return pl.pallas_call(
        expand_kernel,
        grid=(3,),
        in_specs=[pl.BlockSpec((rows, depth), lambda j: (0, j))]
        + [pl.BlockSpec(block.shape, lambda j: (0, 0)) for block in (*own, *other)]
        + [total] * len(early),
        out_specs=total,
        out_shape=jax.ShapeDtypeStruct((rows, width), jnp.float32),
        cost_estimate=pl.CostEstimate(
            flops=2 * rows * depth * width,
            bytes_accessed=(2 * depth + 4 * rows) * width,
            transcendentals=0,
        ),
        compiler_params=pltpu.CompilerParams(vmem_limit_bytes=24 * 1024 * 1024),
        name="expand",
    )(basis_rows, *own, *other, *early)


def shards(tokens, grad_out, projection_basis, first_moment, second_moment):
    dp, outer = lax.axis_index("dp"), lax.axis_index("outer")
    f32, bf16 = jnp.float32, jnp.bfloat16

    places = jnp.concatenate([rank_order(bits, dp, outer) for bits in BITS])
    picks = (lax.broadcasted_iota(jnp.int32, (512, 1536), 0) == places[None, :]).astype(bf16)

    projected = project(tokens, projection_basis)
    projected = jnp.dot(projected, picks, preferred_element_type=f32).astype(bf16)

    local_width = projection_basis.shape[0] // 32
    basis_rows = lax.dynamic_slice_in_dim(projection_basis, dp * local_width, local_width, 0)
    projected, basis_rows = lax.optimization_barrier((projected, basis_rows))

    own, other = [], []
    for piece, (start, size) in enumerate(PIECES):
        terms = lax.dot_general(
            projected[:, 512 * piece : 512 * piece + 512],
            grad_out[:, start : start + size],
            (((0,), (0,)), ((), ())),
            preferred_element_type=f32,
        ).astype(bf16)
        own.append(terms[:256])
        other.append(terms[256:])
    sent = [o[128:].astype(f32) + send(t[128:], SWAP).astype(f32) for o, t in zip(own, other)]
    held = [o[:128].astype(f32) + send(t[:128], SWAP).astype(f32) for o, t in zip(own, other)]
    for level in range(3):
        got = send_pieces([s.astype(bf16) for s in sent], level)
        if level == 0:
            basis_rows = jnp.dot(basis_rows, picks, preferred_element_type=f32).astype(bf16)
            starts = range(0, 1536, 256)
            early_basis = jnp.concatenate([basis_rows[:, at : at + 128] for at in starts], axis=1)
            late_basis = jnp.concatenate([basis_rows[:, at + 128 : at + 256] for at in starts], axis=1)
            got, early_basis, late_basis = lax.optimization_barrier((got, early_basis, late_basis))
        held = [h + g.astype(f32) for h, g in zip(held, got)]
        half = held[0].shape[0] // 2
        if level < 2:
            sent, held = [h[half:] for h in held], [h[:half] for h in held]
    held = jnp.concatenate(held, axis=1)
    terms = swap_groups(held.astype(bf16).reshape(8, 4, -1))
    owned_grad = jnp.sum(terms.astype(f32), axis=0)

    new_first = beta_first * first_moment + (1.0 - beta_first) * owned_grad
    new_second = beta_second * second_moment + (1.0 - beta_second) * owned_grad * owned_grad
    first_bias = 1.0 - beta_first**STEP
    second_bias = 1.0 - beta_second**STEP
    low_update = (new_first / first_bias / (jnp.sqrt(new_second / second_bias) + epsilon)).astype(bf16)

    low = swap_groups(jnp.broadcast_to(low_update[None], (8, *low_update.shape)))
    low = low.reshape(32, -1)
    low = [low[:, start : start + size] for start, size in PIECES]
    for level in (2, 1):
        got = send_pieces(low, level)
        low = [jnp.concatenate([mine, theirs], axis=0) for mine, theirs in zip(low, got)]
    late = send_pieces(low, 0)
    early = expand(early_basis, low, [send(part, SWAP) for part in low])
    weight_update = expand(late_basis, late, [send(part, SWAP) for part in late], early)
    return (weight_update, new_first, new_second)


def solution(mesh):
    in_specs = (
        P(("dp", "outer"), None),
        P(("dp", "outer"), None),
        P(),
        P(("dp", "outer"), None),
        P(("dp", "outer"), None),
    )
    out_specs = (P("dp", None), P(("dp", "outer"), None), P(("dp", "outer"), None))
    return jax.shard_map(shards, mesh=mesh, in_specs=in_specs, out_specs=out_specs, check_vma=False)
```

```python
import itertools

import jax
import jax.numpy as jnp
from jax import lax
from jax.experimental import pallas as pl
from jax.experimental.pallas import tpu as pltpu
from jax.sharding import PartitionSpec as P

STEP = 100

beta_first = 0.9
beta_second = 0.999
epsilon = 1e-08
galore_scale = 0.25

AXES = ("dp", "outer")
WIDTH = 3840
PIECES = ((0, 3840), (3840, 3840), (7680, 3328))
X, Y, Z = 0, 1, 2
BITS = (
    ((X, 0), (Z, 0), (Y, 0)),
    ((Y, 0), (X, 0), (Z, 0)),
    ((Z, 0), (Y, 0), (X, 0)),
)
LAST = ((X, 1), (Y, 1), (Z, 1))


def linear(x, y, z, core):
    return (((x * 2 + y % 2) * 4 + z) * 2 + y // 2) * 2 + core


def code(second, core):
    return 1 + 2 * ((second + core) % 2)


def exchange(*bits):
    pairs = []
    for x, y, z, core in itertools.product(range(4), range(4), range(4), range(2)):
        there = [x, y, z]
        for axis, second in bits:
            there[axis] ^= code(second, core)
        pairs.append((linear(x, y, z, core), linear(*there, core)))
    return pairs


SWAP = [(2 * i + core, 2 * i + 1 - core) for i in range(64) for core in range(2)]


def groups():
    found = []
    for x, y, z, core in itertools.product(range(4), range(4), range(4), range(2)):
        last = code(1, core)
        if all(at < at ^ last for at in (x, y, z)):
            corners = itertools.product((0, last), repeat=3)
            found.append([linear(x ^ dx, y ^ dy, z ^ dz, core) for dx, dy, dz in corners])
    return found


def swap_groups(value):
    return lax.all_to_all(value, AXES, 0, 0, axis_index_groups=groups(), tiled=True)


def send(value, pairs):
    return lax.ppermute(value, AXES, pairs)


def send_pieces(values, level):
    values = lax.optimization_barrier(tuple(values))
    return lax.optimization_barrier(
        tuple(send(v, exchange(bits[level])) for v, bits in zip(values, BITS))
    )


def rank_order(bits, dp, outer):
    here = (dp // 8, (outer // 2) * 2 + (dp // 4) % 2, dp % 4)
    place = lax.iota(jnp.int32, 512)
    core = (outer + place // 256) % 2
    there = list(here)
    for level, (axis, second) in enumerate(bits):
        there[axis] = there[axis] ^ ((place // (128 >> level)) % 2 * code(second, core))
    for level, (axis, second) in enumerate(LAST):
        last = code(second, core)
        first = jnp.minimum(there[axis], there[axis] ^ last)
        there[axis] = first ^ ((place // (16 >> level)) % 2 * last)
    return linear(*there, core) * 4 + place % 4


def project_kernel(at_ref, places_ref, tokens_ref, basis_ref, rows_ref, out_ref, own_rows_ref, total_ref):
    step = pl.program_id(0)
    product = jnp.dot(tokens_ref[...], basis_ref[...], preferred_element_type=jnp.float32)

    @pl.when(step == 0)
    def _():
        total_ref[...] = product
        own_rows_ref[...] = rows_ref[...]

    @pl.when(step > 0)
    def _():
        total_ref[...] += product

    @pl.when(step == pl.num_programs(0) - 1)
    def _():
        projected = total_ref[...].astype(jnp.bfloat16)
        for piece in range(3):
            columns = slice(512 * piece, 512 * piece + 512)
            picks = lax.broadcasted_iota(jnp.int32, (512, 512), 0) == places_ref[:, columns]
            picks = jnp.where(picks, 1.0, 0.0).astype(jnp.bfloat16)
            picked = jnp.dot(projected, picks, preferred_element_type=jnp.float32)
            out_ref[:, columns] = picked.astype(jnp.bfloat16)


def project(at, places, tokens, basis, depth=1024):
    rows, rank, width = tokens.shape[0], basis.shape[1], places.shape[1]
    return pl.pallas_call(
        project_kernel,
        grid_spec=pltpu.PrefetchScalarGridSpec(
            num_scalar_prefetch=1,
            grid=(basis.shape[0] // depth,),
            in_specs=[
                pl.BlockSpec((1, width), lambda k, at: (0, 0)),
                pl.BlockSpec((rows, depth), lambda k, at: (0, k)),
                pl.BlockSpec((depth, rank), lambda k, at: (k, 0)),
                pl.BlockSpec((128, rank), lambda k, at: (at[0], 0)),
            ],
            out_specs=[
                pl.BlockSpec((rows, width), lambda k, at: (0, 0)),
                pl.BlockSpec((128, rank), lambda k, at: (0, 0)),
            ],
            scratch_shapes=[pltpu.VMEM((rows, rank), jnp.float32)],
        ),
        out_shape=[
            jax.ShapeDtypeStruct((rows, width), jnp.bfloat16),
            jax.ShapeDtypeStruct((128, rank), jnp.bfloat16),
        ],
        cost_estimate=pl.CostEstimate(
            flops=2 * rows * (basis.shape[0] + width) * rank,
            bytes_accessed=2 * (rows + rank) * basis.shape[0],
            transcendentals=0,
        ),
        compiler_params=pltpu.CompilerParams(vmem_limit_bytes=12 * 1024 * 1024),
        name="project",
    )(at, places, tokens, basis, basis)


def expand_kernel(basis_ref, *refs):
    for piece in range(3):

        @pl.when(pl.program_id(0) == piece)
        def _(piece=piece):
            size = PIECES[piece][1]
            low = jnp.concatenate([refs[piece][...], refs[3 + piece][...]], axis=0)
            product = jnp.dot(basis_ref[...], low, preferred_element_type=jnp.float32)
            if len(refs) == 8:
                product = -galore_scale * (refs[6][:, :size] + product)
            refs[-1][:, :size] = product


def expand(basis_rows, own, other, *early):
    rows, depth, width = basis_rows.shape[0], 2 * own[0].shape[0], sum(size for _, size in PIECES)
    total = pl.BlockSpec((rows, WIDTH), lambda j: (0, j))
    return pl.pallas_call(
        expand_kernel,
        grid=(3,),
        in_specs=[pl.BlockSpec((rows, depth), lambda j: (0, j))]
        + [pl.BlockSpec(block.shape, lambda j: (0, 0)) for block in (*own, *other)]
        + [total] * len(early),
        out_specs=total,
        out_shape=jax.ShapeDtypeStruct((rows, width), jnp.float32),
        cost_estimate=pl.CostEstimate(
            flops=2 * rows * depth * width,
            bytes_accessed=(2 * depth + 4 * rows) * width,
            transcendentals=0,
        ),
        compiler_params=pltpu.CompilerParams(vmem_limit_bytes=24 * 1024 * 1024),
        name="expand",
    )(basis_rows, *own, *other, *early)


def late_kernel(basis_ref, own_ref, other_ref, early_ref, *refs):
    low = jnp.concatenate([own_ref[...], other_ref[...]], axis=0)
    product = jnp.dot(basis_ref[...], low, preferred_element_type=jnp.float32)
    refs[-1][...] = -galore_scale * (early_ref[...] + product)


def expand_late(piece, basis_rows, own, other, early, *done):
    rows, half, (start, size) = basis_rows.shape[0], own.shape[0], PIECES[piece]
    step = WIDTH // 2
    total = pl.BlockSpec((rows, step), lambda j: (0, start // step + j))
    return pl.pallas_call(
        late_kernel,
        grid=(2,),
        in_specs=[pl.BlockSpec((rows, 2 * half), lambda j: (0, piece))]
        + [pl.BlockSpec((half, step), lambda j: (0, j))] * 2
        + [total]
        + [pl.BlockSpec(memory_space=pl.ANY)] * len(done),
        out_specs=total,
        out_shape=jax.ShapeDtypeStruct(early.shape, jnp.float32),
        input_output_aliases={4: 0} if done else {},
        cost_estimate=pl.CostEstimate(
            flops=4 * rows * half * size,
            bytes_accessed=(4 * half + 8 * rows) * size,
            transcendentals=0,
        ),
        compiler_params=pltpu.CompilerParams(vmem_limit_bytes=16 * 1024 * 1024),
        name="expand_late",
    )(basis_rows, own, other, early, *done)


def shards(tokens, grad_out, projection_basis, first_moment, second_moment):
    dp, outer = lax.axis_index("dp"), lax.axis_index("outer")
    f32, bf16 = jnp.float32, jnp.bfloat16

    places = jnp.concatenate([rank_order(bits, dp, outer) for bits in BITS])
    picks = (lax.broadcasted_iota(jnp.int32, (512, 1536), 0) == places[None, :]).astype(bf16)

    projected, basis_rows = project(dp.reshape(1), places[None, :], tokens, projection_basis)

    own, other = [], []
    for piece, (start, size) in enumerate(PIECES):
        terms = lax.dot_general(
            projected[:, 512 * piece : 512 * piece + 512],
            grad_out[:, start : start + size],
            (((0,), (0,)), ((), ())),
            preferred_element_type=f32,
        ).astype(bf16)
        own.append(terms[:256])
        other.append(terms[256:])
    halves = [[send(t[128:], SWAP), send(t[:128], SWAP)] for t in other[:2]]
    whole = send(other[2], SWAP)
    halves.append([whole[128:], whole[:128]])
    sent = [o[128:].astype(f32) + t[0].astype(f32) for o, t in zip(own, halves)]
    held = [o[:128].astype(f32) + t[1].astype(f32) for o, t in zip(own, halves)]
    for level in range(3):
        got = send_pieces([s.astype(bf16) for s in sent], level)
        if level == 0:
            basis_rows = jnp.dot(basis_rows, picks, preferred_element_type=f32).astype(bf16)
            starts = range(0, 1536, 256)
            early_basis = jnp.concatenate([basis_rows[:, at : at + 128] for at in starts], axis=1)
            late_basis = jnp.concatenate([basis_rows[:, at + 128 : at + 256] for at in starts], axis=1)
            got, early_basis, late_basis = lax.optimization_barrier((got, early_basis, late_basis))
        held = [h + g.astype(f32) for h, g in zip(held, got)]
        half = held[0].shape[0] // 2
        if level < 2:
            sent, held = [h[half:] for h in held], [h[:half] for h in held]
    held = jnp.concatenate(held, axis=1)
    terms = swap_groups(held.astype(bf16).reshape(8, 4, -1))
    owned_grad = jnp.sum(terms.astype(f32), axis=0)

    new_first = beta_first * first_moment + (1.0 - beta_first) * owned_grad
    new_second = beta_second * second_moment + (1.0 - beta_second) * owned_grad * owned_grad
    first_bias = 1.0 - beta_first**STEP
    second_bias = 1.0 - beta_second**STEP
    low_update = (new_first / first_bias / (jnp.sqrt(new_second / second_bias) + epsilon)).astype(bf16)

    low = swap_groups(jnp.broadcast_to(low_update[None], (8, *low_update.shape)))
    low = low.reshape(32, -1)
    low = [low[:, start : start + size] for start, size in PIECES]
    for level in (2, 1):
        got = send_pieces(low, level)
        low = [jnp.concatenate([mine, theirs], axis=0) for mine, theirs in zip(low, got)]
    late = send_pieces(low, 0)
    early = expand(early_basis, low, [send(part, SWAP) for part in low])
    others, done = [send(part, SWAP) for part in late], ()
    for piece in range(3):
        done = (expand_late(piece, late_basis, late[piece], others[piece], early, *done),)
    weight_update = done[0]
    return (weight_update, new_first, new_second)


def solution(mesh):
    in_specs = (
        P(("dp", "outer"), None),
        P(("dp", "outer"), None),
        P(),
        P(("dp", "outer"), None),
        P(("dp", "outer"), None),
    )
    out_specs = (P("dp", None), P(("dp", "outer"), None), P(("dp", "outer"), None))
    return jax.shard_map(shards, mesh=mesh, in_specs=in_specs, out_specs=out_specs, check_vma=False)
```

```python
import itertools

import jax
import jax.numpy as jnp
from jax import lax
from jax.experimental import pallas as pl
from jax.experimental.pallas import tpu as pltpu
from jax.sharding import PartitionSpec as P

STEP = 100

beta_first = 0.9
beta_second = 0.999
epsilon = 1e-08
galore_scale = 0.25

AXES = ("dp", "outer")
WIDTH = 1920
PIECES = ((0, 3840), (3840, 3840), (7680, 3328))
X, Y, Z = 0, 1, 2
BITS = (
    ((X, 0), (Z, 0), (Y, 0)),
    ((Y, 0), (X, 0), (Z, 0)),
    ((Z, 0), (Y, 0), (X, 0)),
)
LAST = ((X, 1), (Y, 1), (Z, 1))


def linear(x, y, z, core):
    return (((x * 2 + y % 2) * 4 + z) * 2 + y // 2) * 2 + core


def code(second, core):
    return 1 + 2 * ((second + core) % 2)


def exchange(*bits):
    pairs = []
    for x, y, z, core in itertools.product(range(4), range(4), range(4), range(2)):
        there = [x, y, z]
        for axis, second in bits:
            there[axis] ^= code(second, core)
        pairs.append((linear(x, y, z, core), linear(*there, core)))
    return pairs


SWAP = [(2 * i + core, 2 * i + 1 - core) for i in range(64) for core in range(2)]


def groups():
    found = []
    for x, y, z, core in itertools.product(range(4), range(4), range(4), range(2)):
        last = code(1, core)
        if all(at < at ^ last for at in (x, y, z)):
            corners = itertools.product((0, last), repeat=3)
            found.append([linear(x ^ dx, y ^ dy, z ^ dz, core) for dx, dy, dz in corners])
    return found


def swap_groups(value):
    return lax.all_to_all(value, AXES, 0, 0, axis_index_groups=groups(), tiled=True)


def send(value, pairs):
    return lax.ppermute(value, AXES, pairs)


def send_pieces(values, level):
    values = lax.optimization_barrier(tuple(values))
    return lax.optimization_barrier(
        tuple(send(v, exchange(bits[level])) for v, bits in zip(values, BITS))
    )


def rank_order(bits, dp, outer):
    here = (dp // 8, (outer // 2) * 2 + (dp // 4) % 2, dp % 4)
    place = lax.iota(jnp.int32, 512)
    core = (outer + place // 256) % 2
    there = list(here)
    for level, (axis, second) in enumerate(bits):
        there[axis] = there[axis] ^ ((place // (128 >> level)) % 2 * code(second, core))
    for level, (axis, second) in enumerate(LAST):
        last = code(second, core)
        first = jnp.minimum(there[axis], there[axis] ^ last)
        there[axis] = first ^ ((place // (16 >> level)) % 2 * last)
    return linear(*there, core) * 4 + place % 4


def project_kernel(at_ref, places_ref, tokens_ref, basis_ref, rows_ref, out_ref, own_rows_ref, total_ref):
    step = pl.program_id(0)
    product = jnp.dot(tokens_ref[...], basis_ref[...], preferred_element_type=jnp.float32)

    @pl.when(step == 0)
    def _():
        total_ref[...] = product
        own_rows_ref[...] = rows_ref[...]

    @pl.when(step > 0)
    def _():
        total_ref[...] += product

    @pl.when(step == pl.num_programs(0) - 1)
    def _():
        projected = total_ref[...].astype(jnp.bfloat16)
        for piece in range(3):
            columns = slice(512 * piece, 512 * piece + 512)
            picks = lax.broadcasted_iota(jnp.int32, (512, 512), 0) == places_ref[:, columns]
            picks = jnp.where(picks, 1.0, 0.0).astype(jnp.bfloat16)
            picked = jnp.dot(projected, picks, preferred_element_type=jnp.float32)
            out_ref[:, columns] = picked.astype(jnp.bfloat16)


def project(at, places, tokens, basis, depth=1024):
    rows, rank, width = tokens.shape[0], basis.shape[1], places.shape[1]
    return pl.pallas_call(
        project_kernel,
        grid_spec=pltpu.PrefetchScalarGridSpec(
            num_scalar_prefetch=1,
            grid=(basis.shape[0] // depth,),
            in_specs=[
                pl.BlockSpec((1, width), lambda k, at: (0, 0)),
                pl.BlockSpec((rows, depth), lambda k, at: (0, k)),
                pl.BlockSpec((depth, rank), lambda k, at: (k, 0)),
                pl.BlockSpec((128, rank), lambda k, at: (at[0], 0)),
            ],
            out_specs=[
                pl.BlockSpec((rows, width), lambda k, at: (0, 0)),
                pl.BlockSpec((128, rank), lambda k, at: (0, 0)),
            ],
            scratch_shapes=[pltpu.VMEM((rows, rank), jnp.float32)],
        ),
        out_shape=[
            jax.ShapeDtypeStruct((rows, width), jnp.bfloat16),
            jax.ShapeDtypeStruct((128, rank), jnp.bfloat16),
        ],
        cost_estimate=pl.CostEstimate(
            flops=2 * rows * (basis.shape[0] + width) * rank,
            bytes_accessed=2 * (rows + rank) * basis.shape[0],
            transcendentals=0,
        ),
        compiler_params=pltpu.CompilerParams(vmem_limit_bytes=12 * 1024 * 1024),
        name="project",
    )(at, places, tokens, basis, basis)


def expand_kernel(basis_ref, *refs):
    low = jnp.concatenate([ref[...] for ref in refs[:4]], axis=0)
    product = jnp.dot(basis_ref[...], low, preferred_element_type=jnp.float32)
    refs[-1][...] = -galore_scale * product


def expand(piece, basis_rows, blocks, places, width, *done):
    rows, (start, size) = basis_rows.shape[0], PIECES[piece]
    return pl.pallas_call(
        expand_kernel,
        grid=(pl.cdiv(size, WIDTH),),
        in_specs=[pl.BlockSpec((rows, 512), lambda j: (0, piece))]
        + [pl.BlockSpec((128, WIDTH), lambda j, place=place: (place, j)) for place in places]
        + [pl.BlockSpec(memory_space=pl.ANY)] * len(done),
        out_specs=pl.BlockSpec((rows, WIDTH), lambda j: (0, start // WIDTH + j)),
        out_shape=jax.ShapeDtypeStruct((rows, width), jnp.float32),
        input_output_aliases={5: 0} if done else {},
        cost_estimate=pl.CostEstimate(
            flops=2 * rows * 512 * size,
            bytes_accessed=(2 * 512 + 4 * rows) * size,
            transcendentals=0,
        ),
        compiler_params=pltpu.CompilerParams(vmem_limit_bytes=16 * 1024 * 1024),
        name="expand",
    )(basis_rows, *blocks, *done)


def shards(tokens, grad_out, projection_basis, first_moment, second_moment):
    dp, outer = lax.axis_index("dp"), lax.axis_index("outer")
    f32, bf16 = jnp.float32, jnp.bfloat16

    places = jnp.concatenate([rank_order(bits, dp, outer) for bits in BITS])
    picks = (lax.broadcasted_iota(jnp.int32, (512, 1536), 0) == places[None, :]).astype(bf16)

    projected, basis_rows = project(dp.reshape(1), places[None, :], tokens, projection_basis)

    own, other = [], []
    for piece, (start, size) in enumerate(PIECES):
        terms = lax.dot_general(
            projected[:, 512 * piece : 512 * piece + 512],
            grad_out[:, start : start + size],
            (((0,), (0,)), ((), ())),
            preferred_element_type=f32,
        ).astype(bf16)
        own.append(terms[:256])
        other.append(terms[256:])
    halves = [[send(t[128:], SWAP), send(t[:128], SWAP)] for t in other[:2]]
    whole = send(other[2], SWAP)
    halves.append([whole[128:], whole[:128]])
    sent = [o[128:].astype(f32) + t[0].astype(f32) for o, t in zip(own, halves)]
    held = [o[:128].astype(f32) + t[1].astype(f32) for o, t in zip(own, halves)]
    for level in range(3):
        got = send_pieces([s.astype(bf16) for s in sent], level)
        if level == 0:
            basis_rows = jnp.dot(basis_rows, picks, preferred_element_type=f32).astype(bf16)
            starts = [512 * p + 128 * at for p in range(3) for at in (0, 2, 1, 3)]
            basis_rows = jnp.concatenate([basis_rows[:, at : at + 128] for at in starts], axis=1)
            got, basis_rows = lax.optimization_barrier((got, basis_rows))
        held = [h + g.astype(f32) for h, g in zip(held, got)]
        half = held[0].shape[0] // 2
        if level < 2:
            sent, held = [h[half:] for h in held], [h[:half] for h in held]
    held = jnp.concatenate(held, axis=1)
    terms = swap_groups(held.astype(bf16).reshape(8, 4, -1))
    owned_grad = jnp.sum(terms.astype(f32), axis=0)

    new_first = beta_first * first_moment + (1.0 - beta_first) * owned_grad
    new_second = beta_second * second_moment + (1.0 - beta_second) * owned_grad * owned_grad
    first_bias = 1.0 - beta_first**STEP
    second_bias = 1.0 - beta_second**STEP
    low_update = (new_first / first_bias / (jnp.sqrt(new_second / second_bias) + epsilon)).astype(bf16)

    low = swap_groups(jnp.broadcast_to(low_update[None], (8, *low_update.shape)))
    low = low.reshape(32, -1)
    low = [low[:, start : start + size] for start, size in PIECES]
    for level in (2, 1):
        got = send_pieces(low, level)
        low = [jnp.concatenate([mine, theirs], axis=0) for mine, theirs in zip(low, got)]
    late = send_pieces(low, 0)
    pair, third = send(jnp.concatenate(low[:2], axis=0), SWAP), send(low[2], SWAP)
    late, pair, third = lax.optimization_barrier((late, pair, third))
    blocks = [low, [pair, pair, third], late, [send(part, SWAP) for part in late]]
    done = ()
    for piece in range(3):
        parts = [block[piece] for block in blocks]
        places = (0, piece % 2, 0, 0)
        done = (expand(piece, basis_rows, parts, places, grad_out.shape[1], *done),)
    weight_update = done[0]
    return (weight_update, new_first, new_second)


def solution(mesh):
    in_specs = (
        P(("dp", "outer"), None),
        P(("dp", "outer"), None),
        P(),
        P(("dp", "outer"), None),
        P(("dp", "outer"), None),
    )
    out_specs = (P("dp", None), P(("dp", "outer"), None), P(("dp", "outer"), None))
    return jax.shard_map(shards, mesh=mesh, in_specs=in_specs, out_specs=out_specs, check_vma=False)
```

```python
import itertools

import jax
import jax.numpy as jnp
from jax import lax
from jax.experimental import pallas as pl
from jax.experimental.pallas import tpu as pltpu
from jax.sharding import PartitionSpec as P

STEP = 100

beta_first = 0.9
beta_second = 0.999
epsilon = 1e-08
galore_scale = 0.25

AXES = ("dp", "outer")
WIDTH = 1920
PIECES = ((0, 3840), (3840, 3840), (7680, 3328))
X, Y, Z = 0, 1, 2
BITS = (
    ((X, 0), (Z, 0), (Y, 0)),
    ((Y, 0), (X, 0), (Z, 0)),
    ((Z, 0), (Y, 0), (X, 0)),
)
LAST = ((X, 1), (Y, 1), (Z, 1))


def linear(x, y, z, core):
    return (((x * 2 + y % 2) * 4 + z) * 2 + y // 2) * 2 + core


def code(second, core):
    return 1 + 2 * ((second + core) % 2)


def exchange(*bits):
    pairs = []
    for x, y, z, core in itertools.product(range(4), range(4), range(4), range(2)):
        there = [x, y, z]
        for axis, second in bits:
            there[axis] ^= code(second, core)
        pairs.append((linear(x, y, z, core), linear(*there, core)))
    return pairs


SWAP = [(2 * i + core, 2 * i + 1 - core) for i in range(64) for core in range(2)]


def groups():
    found = []
    for x, y, z, core in itertools.product(range(4), range(4), range(4), range(2)):
        last = code(1, core)
        if all(at < at ^ last for at in (x, y, z)):
            corners = itertools.product((0, last), repeat=3)
            found.append([linear(x ^ dx, y ^ dy, z ^ dz, core) for dx, dy, dz in corners])
    return found


def swap_groups(value):
    return lax.all_to_all(value, AXES, 0, 0, axis_index_groups=groups(), tiled=True)


def send(value, pairs):
    return lax.ppermute(value, AXES, pairs)


def send_pieces(values, level):
    values = lax.optimization_barrier(tuple(values))
    return tuple(send(v, exchange(bits[level])) for v, bits in zip(values, BITS))


def rank_order(bits, dp, outer):
    here = (dp // 8, (outer // 2) * 2 + (dp // 4) % 2, dp % 4)
    place = lax.iota(jnp.int32, 512)
    core = (outer + place // 256) % 2
    there = list(here)
    for level, (axis, second) in enumerate(bits):
        there[axis] = there[axis] ^ ((place // (128 >> level)) % 2 * code(second, core))
    for level, (axis, second) in enumerate(LAST):
        last = code(second, core)
        first = jnp.minimum(there[axis], there[axis] ^ last)
        there[axis] = first ^ ((place // (16 >> level)) % 2 * last)
    return linear(*there, core) * 4 + place % 4


def project_kernel(at_ref, places_ref, tokens_ref, basis_ref, rows_ref, out_ref, own_rows_ref, total_ref):
    step = pl.program_id(0)
    product = jnp.dot(tokens_ref[...], basis_ref[...], preferred_element_type=jnp.float32)

    @pl.when(step == 0)
    def _():
        total_ref[...] = product
        own_rows_ref[...] = rows_ref[...]

    @pl.when(step > 0)
    def _():
        total_ref[...] += product

    @pl.when(step == pl.num_programs(0) - 1)
    def _():
        projected = total_ref[...].astype(jnp.bfloat16)
        for piece in range(3):
            columns = slice(512 * piece, 512 * piece + 512)
            picks = lax.broadcasted_iota(jnp.int32, (512, 512), 0) == places_ref[:, columns]
            picks = jnp.where(picks, 1.0, 0.0).astype(jnp.bfloat16)
            picked = jnp.dot(projected, picks, preferred_element_type=jnp.float32)
            out_ref[:, columns] = picked.astype(jnp.bfloat16)


def project(at, places, tokens, basis, depth=1024):
    rows, rank, width = tokens.shape[0], basis.shape[1], places.shape[1]
    return pl.pallas_call(
        project_kernel,
        grid_spec=pltpu.PrefetchScalarGridSpec(
            num_scalar_prefetch=1,
            grid=(basis.shape[0] // depth,),
            in_specs=[
                pl.BlockSpec((1, width), lambda k, at: (0, 0)),
                pl.BlockSpec((rows, depth), lambda k, at: (0, k)),
                pl.BlockSpec((depth, rank), lambda k, at: (k, 0)),
                pl.BlockSpec((128, rank), lambda k, at: (at[0], 0)),
            ],
            out_specs=[
                pl.BlockSpec((rows, width), lambda k, at: (0, 0)),
                pl.BlockSpec((128, rank), lambda k, at: (0, 0)),
            ],
            scratch_shapes=[pltpu.VMEM((rows, rank), jnp.float32)],
        ),
        out_shape=[
            jax.ShapeDtypeStruct((rows, width), jnp.bfloat16),
            jax.ShapeDtypeStruct((128, rank), jnp.bfloat16),
        ],
        cost_estimate=pl.CostEstimate(
            flops=2 * rows * (basis.shape[0] + width) * rank,
            bytes_accessed=2 * (rows + rank) * basis.shape[0],
            transcendentals=0,
        ),
        compiler_params=pltpu.CompilerParams(vmem_limit_bytes=12 * 1024 * 1024),
        name="project",
    )(at, places, tokens, basis, basis)


def expand_kernel(basis_ref, *refs):
    low = jnp.concatenate([ref[...] for ref in refs[:4]], axis=0)
    product = jnp.dot(basis_ref[...], low, preferred_element_type=jnp.float32)
    refs[-1][...] = -galore_scale * product


def expand(piece, basis_rows, blocks, places, width, *done):
    rows, (start, size) = basis_rows.shape[0], PIECES[piece]
    return pl.pallas_call(
        expand_kernel,
        grid=(pl.cdiv(size, WIDTH),),
        in_specs=[pl.BlockSpec((rows, 512), lambda j: (0, piece))]
        + [pl.BlockSpec((128, WIDTH), lambda j, place=place: (place, j)) for place in places]
        + [pl.BlockSpec(memory_space=pl.ANY)] * len(done),
        out_specs=pl.BlockSpec((rows, WIDTH), lambda j: (0, start // WIDTH + j)),
        out_shape=jax.ShapeDtypeStruct((rows, width), jnp.float32),
        input_output_aliases={5: 0} if done else {},
        cost_estimate=pl.CostEstimate(
            flops=2 * rows * 512 * size,
            bytes_accessed=(2 * 512 + 4 * rows) * size,
            transcendentals=0,
        ),
        compiler_params=pltpu.CompilerParams(vmem_limit_bytes=16 * 1024 * 1024),
        name="expand",
    )(basis_rows, *blocks, *done)


def shards(tokens, grad_out, projection_basis, first_moment, second_moment):
    dp, outer = lax.axis_index("dp"), lax.axis_index("outer")
    f32, bf16 = jnp.float32, jnp.bfloat16

    places = jnp.concatenate([rank_order(bits, dp, outer) for bits in BITS])
    picks = (lax.broadcasted_iota(jnp.int32, (512, 1536), 0) == places[None, :]).astype(bf16)

    projected, basis_rows = project(dp.reshape(1), places[None, :], tokens, projection_basis)

    own, other = [], []
    for piece, (start, size) in enumerate(PIECES):
        terms = lax.dot_general(
            projected[:, 512 * piece : 512 * piece + 512],
            grad_out[:, start : start + size],
            (((0,), (0,)), ((), ())),
            preferred_element_type=f32,
        ).astype(bf16)
        own.append(terms[:256])
        other.append(terms[256:])
    halves = [[send(t[128:], SWAP), send(t[:128], SWAP)] for t in other[:2]]
    whole = send(other[2], SWAP)
    halves.append([whole[128:], whole[:128]])
    sent = [o[128:].astype(f32) + t[0].astype(f32) for o, t in zip(own, halves)]
    held = [o[:128].astype(f32) + t[1].astype(f32) for o, t in zip(own, halves)]
    for level in range(3):
        got = send_pieces([s.astype(bf16) for s in sent], level)
        if level == 0:
            basis_rows = jnp.dot(basis_rows, picks, preferred_element_type=f32).astype(bf16)
            starts = [512 * p + 128 * at for p in range(3) for at in (0, 2, 1, 3)]
            basis_rows = jnp.concatenate([basis_rows[:, at : at + 128] for at in starts], axis=1)
        held = [h + g.astype(f32) for h, g in zip(held, got)]
        if level == 0:
            held, basis_rows = lax.optimization_barrier((held, basis_rows))
        half = held[0].shape[0] // 2
        if level < 2:
            sent, held = [h[half:] for h in held], [h[:half] for h in held]
    held = jnp.concatenate(held, axis=1)
    terms = swap_groups(held.astype(bf16).reshape(8, 4, -1))
    owned_grad = jnp.sum(terms.astype(f32), axis=0)

    new_first = beta_first * first_moment + (1.0 - beta_first) * owned_grad
    new_second = beta_second * second_moment + (1.0 - beta_second) * owned_grad * owned_grad
    first_bias = 1.0 - beta_first**STEP
    second_bias = 1.0 - beta_second**STEP
    low_update = (new_first / first_bias / (jnp.sqrt(new_second / second_bias) + epsilon)).astype(bf16)

    low = swap_groups(jnp.broadcast_to(low_update[None], (8, *low_update.shape)))
    low = low.reshape(32, -1)
    low = [low[:, start : start + size] for start, size in PIECES]
    for level in (2, 1):
        got = send_pieces(low, level)
        low = [jnp.concatenate([mine, theirs], axis=0) for mine, theirs in zip(low, got)]
    late = send_pieces(low, 0)
    pair, third = send(jnp.concatenate(low[:2], axis=0), SWAP), send(low[2], SWAP)
    late, pair, third = lax.optimization_barrier((late, pair, third))
    blocks = [low, [pair, pair, third], late, [send(part, SWAP) for part in late]]
    done = ()
    for piece in range(3):
        parts = [block[piece] for block in blocks]
        places = (0, piece % 2, 0, 0)
        done = (expand(piece, basis_rows, parts, places, grad_out.shape[1], *done),)
    weight_update = done[0]
    return (weight_update, new_first, new_second)


def solution(mesh):
    in_specs = (
        P(("dp", "outer"), None),
        P(("dp", "outer"), None),
        P(),
        P(("dp", "outer"), None),
        P(("dp", "outer"), None),
    )
    out_specs = (P("dp", None), P(("dp", "outer"), None), P(("dp", "outer"), None))
    return jax.shard_map(shards, mesh=mesh, in_specs=in_specs, out_specs=out_specs, check_vma=False)
```

```python
import itertools

import jax
import jax.numpy as jnp
from jax import lax
from jax.experimental import pallas as pl
from jax.experimental.pallas import tpu as pltpu
from jax.sharding import PartitionSpec as P

STEP = 100

beta_first = 0.9
beta_second = 0.999
epsilon = 1e-08
galore_scale = 0.25

AXES = ("dp", "outer")
WIDTH = 1920
PIECES = ((0, 3840), (3840, 3840), (7680, 3328))
X, Y, Z = 0, 1, 2
BITS = (
    ((X, 0), (Z, 0), (Y, 0)),
    ((Y, 0), (X, 0), (Z, 0)),
    ((Z, 0), (Y, 0), (X, 0)),
)
LAST = ((X, 1), (Y, 1), (Z, 1))


def linear(x, y, z, core):
    return (((x * 2 + y % 2) * 4 + z) * 2 + y // 2) * 2 + core


def code(second, core):
    return 1 + 2 * ((second + core) % 2)


def exchange(*bits):
    pairs = []
    for x, y, z, core in itertools.product(range(4), range(4), range(4), range(2)):
        there = [x, y, z]
        for axis, second in bits:
            there[axis] ^= code(second, core)
        pairs.append((linear(x, y, z, core), linear(*there, core)))
    return pairs


SWAP = [(2 * i + core, 2 * i + 1 - core) for i in range(64) for core in range(2)]


def groups():
    found = []
    for x, y, z, core in itertools.product(range(4), range(4), range(4), range(2)):
        last = code(1, core)
        if all(at < at ^ last for at in (x, y, z)):
            corners = itertools.product((0, last), repeat=3)
            found.append([linear(x ^ dx, y ^ dy, z ^ dz, core) for dx, dy, dz in corners])
    return found


def swap_groups(value):
    return lax.all_to_all(value, AXES, 0, 0, axis_index_groups=groups(), tiled=True)


def send(value, pairs):
    return lax.ppermute(value, AXES, pairs)


def send_pieces(values, level):
    values = lax.optimization_barrier(tuple(values))
    return tuple(send(v, exchange(bits[level])) for v, bits in zip(values, BITS))


def rank_order(bits, dp, outer):
    here = (dp // 8, (outer // 2) * 2 + (dp // 4) % 2, dp % 4)
    place = lax.iota(jnp.int32, 512)
    core = (outer + place // 256) % 2
    there = list(here)
    for level, (axis, second) in enumerate(bits):
        there[axis] = there[axis] ^ ((place // (128 >> level)) % 2 * code(second, core))
    for level, (axis, second) in enumerate(LAST):
        last = code(second, core)
        first = jnp.minimum(there[axis], there[axis] ^ last)
        there[axis] = first ^ ((place // (16 >> level)) % 2 * last)
    return linear(*there, core) * 4 + place % 4


def project_kernel(at_ref, places_ref, tokens_ref, basis_ref, rows_ref, out_ref, own_rows_ref, total_ref):
    step = pl.program_id(0)
    product = jnp.dot(tokens_ref[...], basis_ref[...], preferred_element_type=jnp.float32)

    @pl.when(step == 0)
    def _():
        total_ref[...] = product
        own_rows_ref[...] = rows_ref[...]

    @pl.when(step > 0)
    def _():
        total_ref[...] += product

    @pl.when(step == pl.num_programs(0) - 1)
    def _():
        projected = total_ref[...].astype(jnp.bfloat16)
        for piece in range(3):
            columns = slice(512 * piece, 512 * piece + 512)
            picks = lax.broadcasted_iota(jnp.int32, (512, 512), 0) == places_ref[:, columns]
            picks = jnp.where(picks, 1.0, 0.0).astype(jnp.bfloat16)
            picked = jnp.dot(projected, picks, preferred_element_type=jnp.float32)
            out_ref[:, columns] = picked.astype(jnp.bfloat16)


def project(at, places, tokens, basis, depth=1024):
    rows, rank, width = tokens.shape[0], basis.shape[1], places.shape[1]
    return pl.pallas_call(
        project_kernel,
        grid_spec=pltpu.PrefetchScalarGridSpec(
            num_scalar_prefetch=1,
            grid=(basis.shape[0] // depth,),
            in_specs=[
                pl.BlockSpec((1, width), lambda k, at: (0, 0)),
                pl.BlockSpec((rows, depth), lambda k, at: (0, k)),
                pl.BlockSpec((depth, rank), lambda k, at: (k, 0)),
                pl.BlockSpec((128, rank), lambda k, at: (at[0], 0)),
            ],
            out_specs=[
                pl.BlockSpec((rows, width), lambda k, at: (0, 0)),
                pl.BlockSpec((128, rank), lambda k, at: (0, 0)),
            ],
            scratch_shapes=[pltpu.VMEM((rows, rank), jnp.float32)],
        ),
        out_shape=[
            jax.ShapeDtypeStruct((rows, width), jnp.bfloat16),
            jax.ShapeDtypeStruct((128, rank), jnp.bfloat16),
        ],
        cost_estimate=pl.CostEstimate(
            flops=2 * rows * (basis.shape[0] + width) * rank,
            bytes_accessed=2 * (rows + rank) * basis.shape[0],
            transcendentals=0,
        ),
        compiler_params=pltpu.CompilerParams(vmem_limit_bytes=12 * 1024 * 1024),
        name="project",
    )(at, places, tokens, basis, basis)


def expand_kernel(basis_ref, *refs):
    low = jnp.concatenate([ref[...] for ref in refs[:4]], axis=0)
    product = jnp.dot(basis_ref[...], low, preferred_element_type=jnp.float32)
    refs[-1][...] = -galore_scale * product


def expand(piece, basis_rows, blocks, places, width, *done):
    rows, (start, size) = basis_rows.shape[0], PIECES[piece]
    return pl.pallas_call(
        expand_kernel,
        grid=(pl.cdiv(size, WIDTH),),
        in_specs=[pl.BlockSpec((rows, 512), lambda j: (0, piece))]
        + [pl.BlockSpec((128, WIDTH), lambda j, place=place: (place, j)) for place in places]
        + [pl.BlockSpec(memory_space=pl.ANY)] * len(done),
        out_specs=pl.BlockSpec((rows, WIDTH), lambda j: (0, start // WIDTH + j)),
        out_shape=jax.ShapeDtypeStruct((rows, width), jnp.float32),
        input_output_aliases={5: 0} if done else {},
        cost_estimate=pl.CostEstimate(
            flops=2 * rows * 512 * size,
            bytes_accessed=(2 * 512 + 4 * rows) * size,
            transcendentals=0,
        ),
        compiler_params=pltpu.CompilerParams(vmem_limit_bytes=16 * 1024 * 1024),
        name="expand",
    )(basis_rows, *blocks, *done)


def shards(tokens, grad_out, projection_basis, first_moment, second_moment):
    dp, outer = lax.axis_index("dp"), lax.axis_index("outer")
    f32, bf16 = jnp.float32, jnp.bfloat16

    places = jnp.concatenate([rank_order(bits, dp, outer) for bits in BITS])
    picks = (lax.broadcasted_iota(jnp.int32, (512, 1536), 0) == places[None, :]).astype(bf16)

    projected, basis_rows = project(dp.reshape(1), places[None, :], tokens, projection_basis)

    own, other = [], []
    for piece, (start, size) in enumerate(PIECES):
        terms = lax.dot_general(
            projected[:, 512 * piece : 512 * piece + 512],
            grad_out[:, start : start + size],
            (((0,), (0,)), ((), ())),
            preferred_element_type=f32,
        ).astype(bf16)
        own.append(terms[:256])
        other.append(terms[256:])
    halves = [[send(t[128:], SWAP), send(t[:128], SWAP)] for t in other[:2]]
    whole = send(other[2], SWAP)
    halves.append([whole[128:], whole[:128]])
    sent = [o[128:].astype(f32) + t[0].astype(f32) for o, t in zip(own, halves)]
    held = [o[:128].astype(f32) + t[1].astype(f32) for o, t in zip(own, halves)]
    for level in range(3):
        got = send_pieces([s.astype(bf16) for s in sent], level)
        if level == 0:
            basis_rows = jnp.dot(basis_rows, picks, preferred_element_type=f32).astype(bf16)
            starts = [512 * p + 128 * at for p in range(3) for at in (0, 2, 1, 3)]
            basis_rows = jnp.concatenate([basis_rows[:, at : at + 128] for at in starts], axis=1)
        held = [h + g.astype(f32) for h, g in zip(held, got)]
        if level == 0:
            held, basis_rows = lax.optimization_barrier((held, basis_rows))
        half = held[0].shape[0] // 2
        if level < 2:
            sent, held = [h[half:] for h in held], [h[:half] for h in held]
    held = jnp.concatenate(held, axis=1)
    terms = swap_groups(held.astype(bf16).reshape(8, 4, -1))
    owned_grad = jnp.sum(terms.astype(f32), axis=0)

    new_first = beta_first * first_moment + (1.0 - beta_first) * owned_grad
    new_second = beta_second * second_moment + (1.0 - beta_second) * owned_grad * owned_grad
    first_bias = 1.0 - beta_first**STEP
    second_bias = 1.0 - beta_second**STEP
    low_update = (new_first / first_bias / (jnp.sqrt(new_second / second_bias) + epsilon)).astype(bf16)

    low = swap_groups(jnp.broadcast_to(low_update[None], (8, *low_update.shape)))
    low = low.reshape(32, -1)
    low = [low[:, start : start + size] for start, size in PIECES]
    for level in (2, 1):
        got = send_pieces(low, level)
        low = [jnp.concatenate([mine, theirs], axis=0) for mine, theirs in zip(low, got)]
    late = send_pieces(low, 0)
    pair, third = send(jnp.concatenate(low[:2], axis=0), SWAP), send(low[2], SWAP)
    first, second, last = late
    first, second, pair = lax.optimization_barrier((first, second, pair))
    last, third = lax.optimization_barrier((last, third))
    late = (first, second, last)
    blocks = [low, [pair, pair, third], late, [send(part, SWAP) for part in late]]
    done = ()
    for piece in range(3):
        parts = [block[piece] for block in blocks]
        places = (0, piece % 2, 0, 0)
        done = (expand(piece, basis_rows, parts, places, grad_out.shape[1], *done),)
    weight_update = done[0]
    return (weight_update, new_first, new_second)


def solution(mesh):
    in_specs = (
        P(("dp", "outer"), None),
        P(("dp", "outer"), None),
        P(),
        P(("dp", "outer"), None),
        P(("dp", "outer"), None),
    )
    out_specs = (P("dp", None), P(("dp", "outer"), None), P(("dp", "outer"), None))
    return jax.shard_map(shards, mesh=mesh, in_specs=in_specs, out_specs=out_specs, check_vma=False)
```
